512 devices in a mesh: rep: 64 (over z_hi, y, x), fsdp: 8 (over z_lo, core).
Axes of the slice: x: 4, y: 4, z: 16 (z_hi: 4, z_lo: 4; z = z_hi * 4 + z_lo), core: 2. Of those that a mesh axis runs over, the one named last changes fastest.
Arguments:
- attention_output_features: bfloat16 [131072, 2048], P(('rep', 'fsdp')), may hold values from -6 to 6
- resid: bfloat16 [131072, 4096], P(('rep', 'fsdp')), may hold values from -6 to 6
- adapter_down_weight: float32 [64, 64, 2048], P('rep', None, 'fsdp'), may hold values from -0.125 to 0.125
- adapter_up_weight: float32 [64, 64, 4096], P('rep', None, 'fsdp'), may hold values from -0.75 to 0.75
- adapter_down_moment: float32 [64, 64, 2048], P('rep', None, 'fsdp'), may hold values from -0.15625 to 0.15625
- adapter_down_variance: float32 [64, 64, 2048], P('rep', None, 'fsdp'), may hold values from 1e-06 to 0.0001
- adapter_up_moment: float32 [64, 64, 4096], P('rep', None, 'fsdp'), may hold values from -0.15625 to 0.15625
- adapter_up_variance: float32 [64, 64, 4096], P('rep', None, 'fsdp'), may hold values from 1e-06 to 0.0001
- lengths: int32 [512], P(('rep', 'fsdp')), may hold values from 64 to 256, as said below
- ranks: int32 [64, 8], P('rep'), may hold values from 0 to 7, each once within a row
- gain: bfloat16 [4096], replicated, may hold values from 0.5 to 1.5
- head: float32 [4096], replicated, may hold values from -0.06875 to 0.06875
- step: int32 [1], replicated, may hold values from 0 to 999
Outputs:
- new_lora_a: float32 [64, 64, 2048], P('rep', None, 'fsdp')
- new_lora_b: float32 [64, 64, 4096], P('rep', None, 'fsdp')
- new_moment_a: float32 [64, 64, 2048], P('rep', None, 'fsdp')
- new_second_a: float32 [64, 64, 2048], P('rep', None, 'fsdp')
- new_moment_b: float32 [64, 64, 4096], P('rep', None, 'fsdp')
- new_second_b: float32 [64, 64, 4096], P('rep', None, 'fsdp')
- loss: float32 [64], P('rep')
The draws below stay inside these ranges and needn't reach their ends.
Inputs may be any that keep to these rules, and one draw needn't show every extreme that they name: `lengths`: each prompt's list holds at least one response of exactly 256 valid tokens.
All inputs are finite; a program needn't handle non-finite values.
Results may differ from the reference program's by a relative error of at most 0.0027.
Values may be sent and summed in bfloat16 or wider, within the bound.
No kernel may reach another device: no remote copies, remote signals or barrier semaphores. Data moves between devices by JAX's collectives and lax.ppermute only.
A program may use at most 64 MiB of HBM per device.

```python
import math
import jax
import jax.numpy as jnp
from jax import lax

MODEL_WIDTH = 4096
HALF_HEAD_WIDTH = 2048
ADAPTER_RANK = 64
LIST = 8
PROMPTS = 1
LEN = 256
REPLICA_COUNT = 64
ROWS = 131072


def shared_direction(key):
    return jnp.clip(jax.random.normal(key, (MODEL_WIDTH,), jnp.float32), -4.0, 4.0)


def draw_head(key, part):
    direction = shared_direction(key)
    key = jax.random.fold_in(key, 13)
    factor = jax.random.uniform(key, (MODEL_WIDTH,), jnp.float32, 0.9, 1.1)
    return (direction * factor * MODEL_WIDTH ** (-0.5)).astype(jnp.float32)


def draw_resid(key, part):
    direction = shared_direction(key)
    key = jax.random.fold_in(key, 11)
    noise_key, level_key = jax.random.split(key, 2)
    noise = jnp.clip(jax.random.normal(noise_key, (ROWS, MODEL_WIDTH), jnp.float32), -6.0, 6.0)
    level = jax.random.uniform(level_key, (ROWS, 1), jnp.float32, -1.0, 1.0)
    return jnp.clip(noise + level * direction[None, :], -6.0, 6.0).astype(jnp.bfloat16)


def draw_lengths(key, part):
    key = jax.random.fold_in(key, 7)
    first_key, second_key = jax.random.split(key)
    groups = REPLICA_COUNT * PROMPTS
    base = jax.random.randint(first_key, (groups, LIST), LEN // 4, LEN + 1)
    longest = jax.random.randint(second_key, (groups, 1), 0, LIST)
    spots = jnp.arange(LIST, dtype=jnp.int32)[None, :]
    return jnp.where(spots == longest, LEN, base).reshape(-1).astype(jnp.int32)


def block_levels(key, shape, cuts, smallest, top_value):
    loudness, own = 1.0, jax.random.fold_in(key, 6)
    for dim, blocks in cuts:
        heights = jnp.exp(jax.random.uniform(jax.random.fold_in(own, dim), (blocks,), jnp.float32, smallest / len(cuts), top_value / len(cuts)))
        loudness = loudness * jnp.repeat(heights, shape[dim] // blocks).reshape([-1 if axis == dim else 1 for axis in range(len(shape))])
    return loudness


def scatter_about(own_key, extent, scale, limit, pieces=(), kind=jnp.bfloat16):
    drawn = jax.random.normal(own_key, extent, jnp.float32) * scale
    if len(pieces) > 0:
        drawn = block_levels(own_key, extent, pieces, -0.22, 0.18) * drawn
    return jnp.clip(drawn, min=-limit, max=limit).astype(kind)


def setup_inputs(seed: int = 0) -> dict:
    key_of = jax.random.split(jax.random.key(seed), 14)
    return {
        "attention_output_features": scatter_about(key_of[0], (ROWS, HALF_HEAD_WIDTH), 1.0, 6.0, ((0, 512),)),
        "resid": draw_resid(jax.random.fold_in(key_of[13], 71), 0),
        "adapter_down_weight": scatter_about(key_of[2], (REPLICA_COUNT, ADAPTER_RANK, HALF_HEAD_WIDTH), HALF_HEAD_WIDTH ** -0.5, 0.125, ((0, 64), (2, 8)), jnp.float32),
        "adapter_up_weight": scatter_about(key_of[3], (REPLICA_COUNT, ADAPTER_RANK, MODEL_WIDTH), ADAPTER_RANK ** -0.5, 0.75, ((0, 64), (2, 8)), jnp.float32),
        "adapter_down_moment": scatter_about(key_of[4], (REPLICA_COUNT, ADAPTER_RANK, HALF_HEAD_WIDTH), 0.01, 0.15625, ((0, 64), (2, 8)), jnp.float32),
        "adapter_down_variance": jnp.clip(jnp.exp(math.log(0.0001) - 4.6051702 * jax.random.uniform(key_of[5], (REPLICA_COUNT, ADAPTER_RANK, HALF_HEAD_WIDTH), jnp.float32) ** block_levels(key_of[5], (REPLICA_COUNT, ADAPTER_RANK, HALF_HEAD_WIDTH), ((0, 64), (2, 8)), -0.2, 0.2)), 9.999999974752427e-07, 0.0001),
        "adapter_up_moment": scatter_about(key_of[6], (REPLICA_COUNT, ADAPTER_RANK, MODEL_WIDTH), 0.01, 0.15625, ((0, 64), (2, 8)), jnp.float32),
        "adapter_up_variance": jnp.clip(jnp.exp(math.log(0.0001) - 4.6051702 * jax.random.uniform(key_of[7], (REPLICA_COUNT, ADAPTER_RANK, MODEL_WIDTH), jnp.float32) ** block_levels(key_of[7], (REPLICA_COUNT, ADAPTER_RANK, MODEL_WIDTH), ((0, 64), (2, 8)), -0.2, 0.2)), 9.999999974752427e-07, 0.0001),
        "lengths": draw_lengths(jax.random.fold_in(key_of[13], 71), 0),
        "ranks": jax.vmap(lambda own: jax.random.permutation(own, LIST))(jax.random.split(key_of[9], (REPLICA_COUNT * PROMPTS))).reshape((REPLICA_COUNT * PROMPTS, LIST)).astype(jnp.int32),
        "gain": jnp.clip(1.0 + 0.1 * jax.random.normal(key_of[10], (MODEL_WIDTH,), jnp.float32), 0.5, 1.5).astype(jnp.bfloat16),
        "head": draw_head(jax.random.fold_in(key_of[13], 71), 0),
        "step": jax.random.randint(key_of[12], (1,), 0, 1000).astype(jnp.int32),
    }


def list_loss(scores, ranking_order):
    ordered = jnp.take_along_axis(scores, ranking_order, axis=1)
    tails = jnp.cumsum(jnp.exp(ordered)[:, ::-1], axis=1)[:, ::-1]
    return jnp.sum(jnp.log(tails) - ordered) / scores.shape[0]

def adamw_optimizer_step(param, moment, second, grad, element_count):
    moment = 0.9 * moment + 0.1 * grad
    second = 0.999 * second + 0.001 * grad * grad
    fix_one = 1.0 - jnp.power(jnp.float32(0.9), element_count)
    fix_two = 1.0 - jnp.power(jnp.float32(0.999), element_count)
    update = moment / fix_one / (jnp.sqrt(second / fix_two) + 1e-08) + 0.01 * param
    return (param - 0.001 * update, moment, second)

def replica_step(list_entries, element_count):
    input_features, random_generator, adapter_down_weight, adapter_up_weight, down_first_moment, down_second_moment, up_first_moment, up_second_moment, response_lengths, ranking_order, gain, head = list_entries
    down_half_precision = adapter_down_weight.astype(jnp.bfloat16)
    up_half_precision = adapter_up_weight.astype(jnp.bfloat16)
    z16 = lax.dot_general(input_features, down_half_precision, (((1,), (1,)), ((), ())), preferred_element_type=jnp.float32).astype(jnp.bfloat16)
    hidden = random_generator.astype(jnp.float32) + jnp.dot(z16, up_half_precision, preferred_element_type=jnp.float32)
    scale = lax.rsqrt(lax.optimization_barrier(jnp.mean(hidden * hidden, axis=1, keepdims=True)) + 1e-05)
    gainf = gain.astype(jnp.float32)
    tok = lax.optimization_barrier(jnp.sum(hidden * scale * gainf * head, axis=1)).reshape(response_lengths.shape[0], -1)
    lensf = response_lengths.astype(jnp.float32)
    valid = (jnp.arange(tok.shape[1], dtype=jnp.int32)[None, :] < response_lengths[:, None]).astype(jnp.float32)
    scores = lax.optimization_barrier(jnp.sum(tok * valid, axis=1)) / lensf
    loss, pull = jax.vjp(lambda s: list_loss(s.reshape(ranking_order.shape), ranking_order), scores)
    dscore = pull(jnp.float32(1.0))[0]
    dtok = (dscore[:, None] * valid / lensf[:, None]).reshape(-1, 1)
    weighted = dtok * head * gainf
    dh16 = (scale * weighted - hidden * scale ** 3 * lax.optimization_barrier(jnp.mean(hidden * weighted, axis=1, keepdims=True))).astype(jnp.bfloat16)
    up_gradient = lax.dot_general(z16, dh16, (((0,), (0,)), ((), ())), preferred_element_type=jnp.float32)
    dz16 = lax.dot_general(dh16, up_half_precision, (((1,), (1,)), ((), ())), preferred_element_type=jnp.float32).astype(jnp.bfloat16)
    down_gradient = lax.dot_general(dz16, input_features, (((0,), (0,)), ((), ())), preferred_element_type=jnp.float32)
    updated_down_weight, down_first_moment, down_second_moment = adamw_optimizer_step(adapter_down_weight, down_first_moment, down_second_moment, down_gradient, element_count)
    updated_up_weight, up_first_moment, up_second_moment = adamw_optimizer_step(adapter_up_weight, up_first_moment, up_second_moment, up_gradient, element_count)
    return (updated_down_weight, updated_up_weight, down_first_moment, down_second_moment, up_first_moment, up_second_moment, loss)

def reference(attention_output_features, resid, adapter_down_weight, adapter_up_weight, adapter_down_moment, adapter_down_variance, adapter_up_moment, adapter_up_variance, lengths, ranks, gain, head, step):
    rows = PROMPTS * LIST * LEN
    input_features = attention_output_features.reshape(REPLICA_COUNT, rows, HALF_HEAD_WIDTH)
    random_generator = resid.reshape(REPLICA_COUNT, rows, MODEL_WIDTH)
    response_lengths = lengths.reshape(REPLICA_COUNT, PROMPTS * LIST)
    ranking_order = ranks.reshape(REPLICA_COUNT, PROMPTS, LIST)
    element_count = (step[0] + 1).astype(jnp.float32)

    def single_replica(list_entries):
        return replica_step(list_entries + (gain, head), element_count)
    step_outcomes = lax.map(single_replica, (input_features, random_generator, adapter_down_weight, adapter_up_weight, adapter_down_moment, adapter_down_variance, adapter_up_moment, adapter_up_variance, response_lengths, ranking_order))
    levels = int(math.log2(REPLICA_COUNT))
    shift_bit = (step[0] % levels).astype(jnp.int32)
    partner = jnp.bitwise_xor(jnp.arange(REPLICA_COUNT, dtype=jnp.int32), jnp.left_shift(jnp.int32(1), shift_bit))
    mixed = [(value + value[partner]) * 0.5 for value in step_outcomes[:6]]
    return (mixed[0], mixed[1], mixed[2], mixed[3], mixed[4], mixed[5], step_outcomes[6])
```

```python
import jax
import jax.numpy as jnp
import numpy as np
from jax import lax
from jax.experimental import pallas as pl
from jax.experimental.pallas import tpu as pltpu
from jax.sharding import PartitionSpec as P

F32 = jnp.float32
BF16 = jnp.bfloat16
RANK = 64
LANES = 128
TAIL = 16
COUNT_BITS = 10
VMEM = pl.BlockSpec(memory_space=pltpu.VMEM)
SMEM = pl.BlockSpec(memory_space=pltpu.SMEM)


def nt(left, right):
    return lax.dot_general(left, right, (((1,), (1,)), ((), ())), preferred_element_type=F32)


def tn(left, right):
    return lax.dot_general(left, right, (((0,), (0,)), ((), ())), preferred_element_type=F32)


def nn(left, right):
    return lax.dot_general(left, right, (((1,), (0,)), ((), ())), preferred_element_type=F32)


def split_two(value):
    high = value.astype(BF16)
    return high, (value - high.astype(F32)).astype(BF16)


def split_three(value):
    high = value.astype(BF16)
    rest = value - high.astype(F32)
    middle = rest.astype(BF16)
    return high, middle, (rest - middle.astype(F32)).astype(BF16)


def fold_rows(stacked):
    half = stacked.shape[0] // 2
    return stacked[:half] + stacked[half:]


def gradient_terms(length_ref, x_ref, r_ref, weights_ref, gain_ref, head_ref, out_ref):
    shards = out_ref.shape[0]
    tokens, width = r_ref.shape
    down_cols = x_ref.shape[1] // shards
    up_cols = width // shards
    w = gain_ref[...].astype(F32) * head_ref[...]
    w_high, w_middle, w_low = split_three(w)
    row = lax.broadcasted_iota(jnp.int32, (TAIL, width), 0)
    w_rows = jnp.where(
        row == 0,
        w_high.astype(F32),
        jnp.where(row == 1, w_middle.astype(F32), jnp.where(row == 2, w_low.astype(F32), 0.0)),
    ).astype(BF16)

    def down(shard):
        return weights_ref[shard % 2, shard // 2, :, :down_cols]

    def up(shard):
        return weights_ref[shard % 2, shard // 2, :, down_cols:]

    z = jnp.zeros((tokens, RANK), F32)
    p_ext = jnp.zeros((tokens, RANK + TAIL), F32)
    gram = jnp.zeros((RANK + TAIL, RANK + TAIL), F32)
    for f in range(shards):
        z += nt(x_ref[:, f * down_cols : (f + 1) * down_cols], down(f))
        cols = slice(f * up_cols, (f + 1) * up_cols)
        b_ext = jnp.concatenate([up(f), w_rows[:, cols]], axis=0)
        p_ext += nt(r_ref[:, cols], b_ext)
        gram += nt(b_ext, b_ext)
    squares = jnp.zeros((tokens, LANES), F32)
    for c in range(width // LANES):
        piece = r_ref[:, c * LANES : (c + 1) * LANES].astype(F32)
        squares += piece * piece
    squares = jnp.sum(squares, axis=1, keepdims=True)

    z16 = z.astype(BF16)
    zf = z16.astype(F32)
    p = p_ext[:, :RANK]
    m_high, m_middle, m_low = split_three(gram[:RANK, :RANK])
    v = p + (nn(z16, m_high) + (nn(z16, m_middle) + nn(z16, m_low)))
    bw = jnp.sum(gram[RANK : RANK + 3, :RANK], axis=0, keepdims=True)
    rw = jnp.sum(p_ext[:, RANK : RANK + 3], axis=1, keepdims=True)
    total = squares + jnp.sum(zf * (p + v), axis=1, keepdims=True)
    along = rw + jnp.sum(zf * bw, axis=1, keepdims=True)
    scale = lax.rsqrt(total * (1.0 / width) + 1e-05)

    length = length_ref[0]
    token = lax.broadcasted_iota(jnp.int32, (tokens, 1), 0)
    over = jnp.where(token < length, 1.0 / jnp.full((tokens, 1), length, jnp.int32).astype(F32), 0.0)
    score = jnp.sum(over * scale * along, axis=0, keepdims=True)
    alpha = over * scale
    beta = over * scale * scale * scale * along * (1.0 / width)

    dz = jnp.concatenate(split_two(alpha * bw - beta * v), axis=1)
    bz = jnp.concatenate(split_two(beta * zf), axis=1)
    az = jnp.concatenate(split_two(alpha * zf), axis=1)
    az_sum = fold_rows(tn(az, jnp.ones((tokens, LANES), BF16)))
    inner = jnp.concatenate(split_two(fold_rows(tn(bz, z16))), axis=0)
    s_high, s_middle, s_low = split_three(jnp.broadcast_to(score, (TAIL, LANES)))
    tail_row = lax.broadcasted_iota(jnp.int32, (TAIL, LANES), 0)
    tail = jnp.where(
        tail_row == 0,
        s_high.astype(F32),
        jnp.where(tail_row == 1, s_middle.astype(F32), s_low.astype(F32)),
    ).astype(BF16)
    for f in range(shards):
        term_a = fold_rows(tn(dz, x_ref[:, f * down_cols : (f + 1) * down_cols])).astype(BF16)
        at = 0
        for c in range(down_cols // LANES):
            out_ref[f, at : at + RANK, :] = term_a[:, c * LANES : (c + 1) * LANES]
            at += RANK
        term_b = fold_rows(
            tn(bz, r_ref[:, f * up_cols : (f + 1) * up_cols]) + nn(inner, up(f))
        )
        for c in range(up_cols // LANES):
            first = f * up_cols + c * LANES
            out_ref[f, at : at + RANK, :] = (
                az_sum * w[:, first : first + LANES] - term_b[:, c * LANES : (c + 1) * LANES]
            ).astype(BF16)
            at += RANK
        out_ref[f, at : at + TAIL, :] = tail


def power_gap(base, count):
    factor = float(np.float32(base))
    gap = jnp.float32(0.0)
    for bit in range(COUNT_BITS):
        part = jnp.float32(1.0 - factor ** (2**bit))
        gap = jnp.where((count >> bit) & 1 == 1, gap + part - gap * part, gap)
    return gap


def update(
    ranks_ref, step_ref, terms_ref, a_ref, ma_ref, va_ref, b_ref, mb_ref, vb_ref,
    na_ref, nma_ref, nva_ref, nb_ref, nmb_ref, nvb_ref, packed_ref, loss_ref,
):
    shards = terms_ref.shape[0]
    base = terms_ref.shape[1] - TAIL
    square = (shards, LANES)
    sublane = lax.broadcasted_iota(jnp.int32, square, 0)
    lane = lax.broadcasted_iota(jnp.int32, square, 1)
    score_col = jnp.zeros(square, F32)
    score_row = jnp.zeros(square, F32)
    place_col = jnp.zeros(square, jnp.int32)
    place_row = jnp.zeros(square, jnp.int32)
    for d in range(shards):
        parts = terms_ref[d, base : base + TAIL, :].astype(F32)
        one = jnp.broadcast_to(parts[0:1] + (parts[1:2] + parts[2:3]), square)
        score_col = jnp.where(sublane == d, one, score_col)
        score_row = jnp.where(lane == d, one, score_row)
        place_col = jnp.where(sublane == ranks_ref[0, d], d, place_col)
        place_row = jnp.where(lane == ranks_ref[0, d], d, place_row)
    live = lane < shards
    after = jnp.where(live & (place_col >= place_row), 1.0, 0.0)
    weight = jnp.exp(score_col)
    tails = jnp.where(live[:1], jnp.sum(after * weight, axis=0, keepdims=True), 1.0)
    losses = jnp.where(live[:1], jnp.log(tails) - score_row[:1], 0.0)
    loss_ref[0] = jnp.sum(losses)
    pull = jnp.sum(after * (weight / tails), axis=1, keepdims=True) - 1.0

    count = step_ref[0] + 1
    one_fix = 1.0 / jnp.full((RANK, LANES), power_gap(0.9, count), F32)
    two_fix = 1.0 / jnp.full((RANK, LANES), power_gap(0.999, count), F32)
    at = 0
    for refs in (
        (a_ref, ma_ref, va_ref, na_ref, nma_ref, nva_ref),
        (b_ref, mb_ref, vb_ref, nb_ref, nmb_ref, nvb_ref),
    ):
        for c in range(refs[0].shape[2] // LANES):
            cols = slice(c * LANES, (c + 1) * LANES)
            grad = jnp.zeros((RANK, LANES), F32)
            for d in range(shards):
                grad += pull[d : d + 1] * terms_ref[d, at : at + RANK, :].astype(F32)
            param = refs[0][0, :, cols]
            moment = 0.9 * refs[1][0, :, cols] + 0.1 * grad
            second = 0.999 * refs[2][0, :, cols] + 0.001 * grad * grad
            change = moment * one_fix / (jnp.sqrt(second * two_fix) + 1e-08) + 0.01 * param
            param = param - 0.001 * change
            for i, value in enumerate((param, moment, second)):
                refs[3 + i][0, :, cols] = value
                packed_ref[i, at : at + RANK, :] = value.astype(BF16)
            at += RANK


def average(theirs_ref, *refs):
    mine, out = refs[:6], refs[6:]
    for i in range(3):
        at = 0
        for array in (i, 3 + i):
            for c in range(mine[array].shape[2] // LANES):
                cols = slice(c * LANES, (c + 1) * LANES)
                out[array][0, :, cols] = 0.5 * (
                    mine[array][0, :, cols] + theirs_ref[i, at : at + RANK, :].astype(F32)
                )
                at += RANK


def partner_swap(bit):

    def swap(packed):
        size = lax.axis_size("rep")
        return lax.ppermute(packed, "rep", [(i, i ^ 1 << bit) for i in range(size)])

    return swap


def gather_weights(packed):
    size = lax.axis_size("fsdp")
    same_core = [list(range(core, size, 2)) for core in range(2)]
    same_chip = [[first, first + 1] for first in range(0, size, 2)]
    across = lax.all_gather(packed, "fsdp", axis_index_groups=same_core)
    return lax.all_gather(across, "fsdp", axis_index_groups=same_chip)


def per_device(
    features, resid, down_weight, up_weight, down_moment, down_variance, up_moment, up_variance,
    lengths, ranks, gain, head, step,
):
    shards = lax.axis_size("fsdp")
    levels = lax.axis_size("rep").bit_length() - 1
    width = resid.shape[1]
    panels = (down_weight.shape[2] + up_weight.shape[2]) // LANES
    packed = jnp.concatenate([down_weight[0], up_weight[0]], axis=1).astype(BF16)
    weights = gather_weights(packed)
    terms = pl.pallas_call(
        gradient_terms,
        out_shape=jax.ShapeDtypeStruct((shards, panels * RANK + TAIL, LANES), BF16),
        in_specs=[SMEM] + [VMEM] * 5,
        out_specs=VMEM,
        compiler_params=pltpu.CompilerParams(vmem_limit_bytes=32 * 2**20),
        name="gradient_terms",
    )(lengths, features, resid, weights, gain.reshape(1, width), head.reshape(1, width))
    terms = lax.all_to_all(terms, "fsdp", 0, 0)
    state = (down_weight, down_moment, down_variance, up_weight, up_moment, up_variance)
    outs = pl.pallas_call(
        update,
        out_shape=[jax.ShapeDtypeStruct(s.shape, F32) for s in state]
        + [
            jax.ShapeDtypeStruct((3, panels * RANK, LANES), BF16),
            jax.ShapeDtypeStruct((1,), F32),
        ],
        in_specs=[SMEM, SMEM] + [VMEM] * 7,
        out_specs=[VMEM] * 7 + [SMEM],
        compiler_params=pltpu.CompilerParams(vmem_limit_bytes=32 * 2**20),
        name="update",
    )(ranks, step, terms, *state)
    mine, mine_packed, loss = outs[:6], outs[6], outs[7]
    theirs = lax.switch(step[0] % levels, [partner_swap(bit) for bit in range(levels)], mine_packed)
    mixed = pl.pallas_call(
        average,
        out_shape=[jax.ShapeDtypeStruct(s.shape, F32) for s in state],
        in_specs=[VMEM] * 7,
        out_specs=[VMEM] * 6,
        compiler_params=pltpu.CompilerParams(vmem_limit_bytes=32 * 2**20),
        name="average",
    )(theirs, *mine)
    new_a, new_ma, new_va, new_b, new_mb, new_vb = mixed
    return new_a, new_b, new_ma, new_va, new_mb, new_vb, loss


def solution(mesh):
    rows = P(("rep", "fsdp"), None)
    cols = P("rep", None, "fsdp")
    in_specs = (rows, rows) + (cols,) * 6 + (P(("rep", "fsdp")), P("rep", None), P(), P(), P())
    out_specs = (cols,) * 6 + (P("rep"),)
    return jax.shard_map(
        per_device, mesh=mesh, in_specs=in_specs, out_specs=out_specs, check_vma=False
    )
```

```python
import jax
import jax.numpy as jnp
import numpy as np
from jax import lax
from jax.experimental import pallas as pl
from jax.experimental.pallas import tpu as pltpu
from jax.sharding import PartitionSpec as P

F32 = jnp.float32
BF16 = jnp.bfloat16
RANK = 64
LANES = 128
TAIL = 16
COUNT_BITS = 10
VMEM = pl.BlockSpec(memory_space=pltpu.VMEM)
SMEM = pl.BlockSpec(memory_space=pltpu.SMEM)


def nt(left, right):
    return lax.dot_general(left, right, (((1,), (1,)), ((), ())), preferred_element_type=F32)


def tn(left, right):
    return lax.dot_general(left, right, (((0,), (0,)), ((), ())), preferred_element_type=F32)


def nn(left, right):
    return lax.dot_general(left, right, (((1,), (0,)), ((), ())), preferred_element_type=F32)


def split_two(value):
    high = value.astype(BF16)
    return high, (value - high.astype(F32)).astype(BF16)


def split_three(value):
    high = value.astype(BF16)
    rest = value - high.astype(F32)
    middle = rest.astype(BF16)
    return high, middle, (rest - middle.astype(F32)).astype(BF16)


def fold_rows(stacked):
    half = stacked.shape[0] // 2
    return stacked[:half] + stacked[half:]


def stage_inputs(x_ref, r_ref, gain_ref, head_ref, x_out_ref, r_out_ref, squares_ref, w_ref, rows_ref):
    x_out_ref[...] = x_ref[...]
    tokens, width = r_ref.shape
    w = gain_ref[...].astype(F32) * head_ref[...]
    w_ref[...] = w
    parts = [part.astype(F32) for part in split_three(w)]
    row = lax.broadcasted_iota(jnp.int32, (TAIL, LANES), 0)
    squares = jnp.zeros((tokens, LANES), F32)
    for c in range(width // LANES):
        cols = slice(c * LANES, (c + 1) * LANES)
        high, middle, low = [part[c : c + 1] for part in parts]
        rows = jnp.where(row == 0, high, jnp.where(row == 1, middle, low))
        rows_ref[:, cols] = jnp.where(row < 3, rows, 0.0).astype(BF16)
        piece = r_ref[:, cols]
        r_out_ref[:, cols] = piece
        squares += piece.astype(F32) * piece.astype(F32)
    squares_ref[...] = jnp.broadcast_to(jnp.sum(squares, axis=1, keepdims=True), (tokens, LANES))


def gradient_terms(length_ref, x_ref, r_ref, weights_ref, squares_ref, w_ref, rows_ref, out_ref):
    shards = out_ref.shape[0]
    tokens, width = r_ref.shape
    down_cols = x_ref.shape[1] // shards
    up_cols = width // shards

    def down(shard):
        return weights_ref[shard % 2, shard // 2, :, :down_cols]

    def up(shard):
        return weights_ref[shard % 2, shard // 2, :, down_cols:]

    z = jnp.zeros((tokens, RANK), F32)
    p_ext = jnp.zeros((tokens, RANK + TAIL), F32)
    gram = jnp.zeros((RANK + TAIL, RANK + TAIL), F32)
    for f in range(shards):
        z += nt(x_ref[:, f * down_cols : (f + 1) * down_cols], down(f))
        cols = slice(f * up_cols, (f + 1) * up_cols)
        b_ext = jnp.concatenate([up(f), rows_ref[:, cols]], axis=0)
        p_ext += nt(r_ref[:, cols], b_ext)
        gram += nt(b_ext, b_ext)
    squares = squares_ref[:, :1]

    z16 = z.astype(BF16)
    zf = z16.astype(F32)
    p = p_ext[:, :RANK]
    m_high, m_middle, m_low = split_three(gram[:RANK, :RANK])
    v = p + (nn(z16, m_high) + (nn(z16, m_middle) + nn(z16, m_low)))
    bw = jnp.sum(gram[RANK : RANK + 3, :RANK], axis=0, keepdims=True)
    rw = jnp.sum(p_ext[:, RANK : RANK + 3], axis=1, keepdims=True)
    total = squares + jnp.sum(zf * (p + v), axis=1, keepdims=True)
    along = rw + jnp.sum(zf * bw, axis=1, keepdims=True)
    scale = lax.rsqrt(total * (1.0 / width) + 1e-05)

    length = length_ref[0]
    token = lax.broadcasted_iota(jnp.int32, (tokens, 1), 0)
    over = jnp.where(token < length, 1.0 / jnp.full((tokens, 1), length, jnp.int32).astype(F32), 0.0)
    score = jnp.sum(over * scale * along, axis=0, keepdims=True)
    alpha = over * scale
    beta = over * scale * scale * scale * along * (1.0 / width)

    dz = jnp.concatenate(split_two(alpha * bw - beta * v), axis=1)
    bz = jnp.concatenate(split_two(beta * zf), axis=1)
    az = jnp.concatenate(split_two(alpha * zf), axis=1)
    az_sum = fold_rows(tn(az, jnp.ones((tokens, LANES), BF16)))
    inner = jnp.concatenate(split_two(fold_rows(tn(bz, z16))), axis=0)
    s_high, s_middle, s_low = split_three(jnp.broadcast_to(score, (TAIL, LANES)))
    tail_row = lax.broadcasted_iota(jnp.int32, (TAIL, LANES), 0)
    tail = jnp.where(
        tail_row == 0,
        s_high.astype(F32),
        jnp.where(tail_row == 1, s_middle.astype(F32), s_low.astype(F32)),
    ).astype(BF16)
    for f in range(shards):
        term_a = fold_rows(tn(dz, x_ref[:, f * down_cols : (f + 1) * down_cols])).astype(BF16)
        at = 0
        for c in range(down_cols // LANES):
            out_ref[f, at : at + RANK, :] = term_a[:, c * LANES : (c + 1) * LANES]
            at += RANK
        term_b = fold_rows(
            tn(bz, r_ref[:, f * up_cols : (f + 1) * up_cols]) + nn(inner, up(f))
        )
        for c in range(up_cols // LANES):
            panel = f * up_cols // LANES + c
            out_ref[f, at : at + RANK, :] = (
                az_sum * w_ref[panel : panel + 1] - term_b[:, c * LANES : (c + 1) * LANES]
            ).astype(BF16)
            at += RANK
        out_ref[f, at : at + TAIL, :] = tail


def power_gap(base, count):
    factor = float(np.float32(base))
    gap = jnp.float32(0.0)
    for bit in range(COUNT_BITS):
        part = jnp.float32(1.0 - factor ** (2**bit))
        gap = jnp.where((count >> bit) & 1 == 1, gap + part - gap * part, gap)
    return gap


def pull_scores(ranks_ref, terms_ref, loss_ref):
    shards = terms_ref.shape[0]
    base = terms_ref.shape[1] - TAIL
    square = (shards, LANES)
    sublane = lax.broadcasted_iota(jnp.int32, square, 0)
    lane = lax.broadcasted_iota(jnp.int32, square, 1)
    score_col = jnp.zeros(square, F32)
    score_row = jnp.zeros(square, F32)
    place_col = jnp.zeros(square, jnp.int32)
    place_row = jnp.zeros(square, jnp.int32)
    for d in range(shards):
        parts = terms_ref[d, base : base + TAIL, :].astype(F32)
        one = jnp.broadcast_to(parts[0:1] + (parts[1:2] + parts[2:3]), square)
        score_col = jnp.where(sublane == d, one, score_col)
        score_row = jnp.where(lane == d, one, score_row)
        place_col = jnp.where(sublane == ranks_ref[0, d], d, place_col)
        place_row = jnp.where(lane == ranks_ref[0, d], d, place_row)
    live = lane < shards
    after = jnp.where(live & (place_col >= place_row), 1.0, 0.0)
    weight = jnp.exp(score_col)
    tails = jnp.where(live[:1], jnp.sum(after * weight, axis=0, keepdims=True), 1.0)
    losses = jnp.where(live[:1], jnp.log(tails) - score_row[:1], 0.0)
    loss_ref[0] = jnp.sum(losses)
    return jnp.sum(after * (weight / tails), axis=1, keepdims=True) - 1.0


def weighed(pull, terms_ref, rows):
    grad = pull[:1] * terms_ref[0, rows, :].astype(F32)
    for d in range(1, terms_ref.shape[0]):
        grad += pull[d : d + 1] * terms_ref[d, rows, :].astype(F32)
    return grad


def adamw(count, grad, param, moment, second):
    one_fix = 1.0 / jnp.full(grad.shape, power_gap(0.9, count), F32)
    two_fix = 1.0 / jnp.full(grad.shape, power_gap(0.999, count), F32)
    moment = 0.9 * moment + 0.1 * grad
    second = 0.999 * second + 0.001 * grad * grad
    change = moment * one_fix / (jnp.sqrt(second * two_fix) + 1e-08) + 0.01 * param
    return param - 0.001 * change, moment, second


def panels_of(refs):
    at = 0
    for first in (0, 3):
        for c in range(refs[first].shape[2] // LANES):
            yield slice(at, at + RANK), first, slice(c * LANES, (c + 1) * LANES)
            at += RANK


def pack_weights(a_ref, b_ref, out_ref):
    cols = a_ref.shape[2]
    for copy in range(out_ref.shape[0]):
        out_ref[copy, :, :cols] = a_ref[0].astype(BF16)
        out_ref[copy, :, cols:] = b_ref[0].astype(BF16)


def pack_state(*refs):
    out_ref = refs[-1]
    for rows, first, cols in panels_of(refs[:6]):
        for i in range(3):
            out_ref[i, rows, :] = refs[first + i][0, :, cols].astype(BF16)


def update(ranks_ref, step_ref, terms_ref, *refs):
    state, out, packed_ref, loss_ref = refs[:6], refs[6:12], refs[12], refs[13]
    pull = pull_scores(ranks_ref, terms_ref, loss_ref)
    for rows, first, cols in panels_of(state):
        grad = weighed(pull, terms_ref, rows)
        old = [state[first + i][0, :, cols] for i in range(3)]
        for i, value in enumerate(adamw(step_ref[0] + 1, grad, *old)):
            out[first + i][0, :, cols] = value
            packed_ref[i, rows, :] = value.astype(BF16)


def average(theirs_ref, *refs):
    mine, out = refs[:6], refs[6:]
    for rows, first, cols in panels_of(mine):
        for i in range(3):
            out[first + i][0, :, cols] = 0.5 * (
                mine[first + i][0, :, cols] + theirs_ref[i, rows, :].astype(F32)
            )


def gradient(ranks_ref, terms_ref, grad_ref, packed_ref, loss_ref):
    pull = pull_scores(ranks_ref, terms_ref, loss_ref)
    for first in range(0, grad_ref.shape[0], RANK):
        rows = slice(first, first + RANK)
        grad = weighed(pull, terms_ref, rows)
        grad_ref[rows, :] = grad
        packed_ref[rows, :] = grad.astype(BF16)


def own_update(step_ref, grad_ref, *refs):
    state, out = refs[:6], refs[6:]
    for rows, first, cols in panels_of(state):
        old = [state[first + i][0, :, cols] for i in range(3)]
        for i, value in enumerate(adamw(step_ref[0] + 1, grad_ref[rows, :], *old)):
            out[first + i][0, :, cols] = value


def their_update(step_ref, grad_ref, state_ref, *refs):
    mine, out = refs[:6], refs[6:]
    for rows, first, cols in panels_of(mine):
        old = [state_ref[i, rows, :].astype(F32) for i in range(3)]
        grad = grad_ref[rows, :].astype(F32)
        for i, value in enumerate(adamw(step_ref[0] + 1, grad, *old)):
            out[first + i][0, :, cols] = 0.5 * (mine[first + i][0, :, cols] + value)


def call(kernel, out_shape, smem, operands, out_specs=None, cost=(0, 0)):
    many = isinstance(out_shape, (list, tuple))
    if out_specs is None:
        out_specs = [VMEM] * len(out_shape) if many else VMEM
    return pl.pallas_call(
        kernel,
        out_shape=out_shape,
        in_specs=[SMEM] * smem + [VMEM] * (len(operands) - smem),
        out_specs=out_specs,
        compiler_params=pltpu.CompilerParams(vmem_limit_bytes=16 * 2**20),
        cost_estimate=pl.CostEstimate(flops=cost[0], bytes_accessed=cost[1], transcendentals=0),
        name=kernel.__name__,
    )(*operands)


def shape(dims, dtype):
    return jax.ShapeDtypeStruct(dims, dtype)


def whole_step(bit, operands):
    (
        features, resid, down_weight, up_weight, down_moment, down_variance, up_moment,
        up_variance, lengths, ranks, gain, head, step,
    ) = operands
    shards = lax.axis_size("fsdp")
    replicas = lax.axis_size("rep")
    swap = [(i, i ^ 1 << bit) for i in range(replicas)]
    cols = down_weight.shape[2] + up_weight.shape[2]
    rows = cols // LANES * RANK
    panels = resid.shape[1] // LANES
    state = (down_weight, down_moment, down_variance, up_weight, up_moment, up_variance)
    kept = [shape(s.shape, F32) for s in state]
    loss_shape = shape((1,), F32)
    same_core = [list(range(core, shards, 2)) for core in range(2)]
    same_chip = [[first, first + 1] for first in range(0, shards, 2)]
    packed = call(
        pack_weights, shape((shards // 2, RANK, cols), BF16), 0, (down_weight, up_weight)
    )
    across = lax.all_to_all(packed, "fsdp", 0, 0, axis_index_groups=same_core)
    tokens, width = resid.shape
    features, resid, squares, w, w_rows = call(
        stage_inputs,
        [
            shape(features.shape, BF16), shape(resid.shape, BF16), shape((tokens, LANES), F32),
            shape((panels, LANES), F32), shape((TAIL, width), BF16),
        ],
        0,
        (features, resid, gain.reshape(panels, LANES), head.reshape(panels, LANES)),
        cost=(tokens * width * 4, tokens * width * 6),
    )
    weights = lax.all_gather(across, "fsdp", axis_index_groups=same_chip)
    terms = call(
        gradient_terms,
        shape((shards, rows + TAIL, LANES), BF16),
        1,
        (lengths, features, resid, weights, squares, w, w_rows),
    )
    terms = lax.all_to_all(terms, "fsdp", 0, 0)
    if replicas >> bit <= 4:
        *mine, packed, loss = call(
            update,
            kept + [shape((3, rows, LANES), BF16), loss_shape],
            2,
            (ranks, step, terms) + state,
            [VMEM] * 7 + [SMEM],
        )
        theirs = lax.ppermute(packed, "rep", swap)
        mixed = call(average, kept, 0, (theirs,) + tuple(mine))
    else:
        old = call(pack_state, shape((3, rows, LANES), BF16), 0, state)
        their_state = lax.ppermute(old, "rep", swap)
        grad, grad16, loss = call(
            gradient,
            [shape((rows, LANES), F32), shape((rows, LANES), BF16), loss_shape],
            1,
            (ranks, terms),
            [VMEM, VMEM, SMEM],
        )
        their_grad = lax.ppermute(grad16, "rep", swap)
        mine = call(
            own_update, kept, 1, (step, grad) + state, cost=(rows * LANES * 40, rows * LANES * 24)
        )
        mixed = call(their_update, kept, 1, (step, their_grad, their_state) + tuple(mine))
    new_a, new_ma, new_va, new_b, new_mb, new_vb = mixed
    return new_a, new_b, new_ma, new_va, new_mb, new_vb, loss


def with_bit(bit):

    def step(operands):
        return whole_step(bit, operands)

    return step


def per_device(*operands):
    levels = lax.axis_size("rep").bit_length() - 1
    step = operands[-1]
    return lax.switch(step[0] % levels, [with_bit(bit) for bit in range(levels)], operands)


def solution(mesh):
    rows = P(("rep", "fsdp"), None)
    cols = P("rep", None, "fsdp")
    in_specs = (rows, rows) + (cols,) * 6 + (P(("rep", "fsdp")), P("rep", None), P(), P(), P())
    out_specs = (cols,) * 6 + (P("rep"),)
    return jax.shard_map(
        per_device, mesh=mesh, in_specs=in_specs, out_specs=out_specs, check_vma=False
    )
```

```python
import jax
import jax.numpy as jnp
import numpy as np
from jax import lax
from jax.experimental import pallas as pl
from jax.experimental.pallas import tpu as pltpu
from jax.sharding import PartitionSpec as P

F32 = jnp.float32
BF16 = jnp.bfloat16
RANK = 64
LANES = 128
TAIL = 16
COUNT_BITS = 10
FAR = 2
VMEM = pl.BlockSpec(memory_space=pltpu.VMEM)
SMEM = pl.BlockSpec(memory_space=pltpu.SMEM)


def nt(left, right):
    return lax.dot_general(left, right, (((1,), (1,)), ((), ())), preferred_element_type=F32)


def tn(left, right):
    return lax.dot_general(left, right, (((0,), (0,)), ((), ())), preferred_element_type=F32)


def nn(left, right):
    return lax.dot_general(left, right, (((1,), (0,)), ((), ())), preferred_element_type=F32)


def split_two(value):
    high = value.astype(BF16)
    return high, (value - high.astype(F32)).astype(BF16)


def split_three(value):
    high = value.astype(BF16)
    rest = value - high.astype(F32)
    middle = rest.astype(BF16)
    return high, middle, (rest - middle.astype(F32)).astype(BF16)


def fold_rows(stacked):
    half = stacked.shape[0] // 2
    return stacked[:half] + stacked[half:]


def prepare(r_ref, gain_ref, head_ref, squares_ref, w_ref, rows_ref):
    tokens, width = r_ref.shape
    w = gain_ref[...].astype(F32) * head_ref[...]
    w_ref[...] = w
    parts = [part.astype(F32) for part in split_three(w)]
    row = lax.broadcasted_iota(jnp.int32, (TAIL, LANES), 0)
    squares = jnp.zeros((tokens, LANES), F32)
    for c in range(width // LANES):
        cols = slice(c * LANES, (c + 1) * LANES)
        high, middle, low = [part[c : c + 1] for part in parts]
        rows = jnp.where(row == 0, high, jnp.where(row == 1, middle, low))
        rows_ref[:, cols] = jnp.where(row < 3, rows, 0.0).astype(BF16)
        piece = r_ref[:, cols].astype(F32)
        squares += piece * piece
    squares_ref[...] = jnp.broadcast_to(jnp.sum(squares, axis=1, keepdims=True), (tokens, LANES))


def gradient_terms(length_ref, x_ref, r_ref, weights_ref, squares_ref, w_ref, rows_ref, out_ref):
    shards = out_ref.shape[0]
    tokens, width = r_ref.shape
    down_cols = x_ref.shape[1] // shards
    up_cols = width // shards

    def down(shard):
        return weights_ref[shard % 2, shard // 2, :, :down_cols]

    def up(shard):
        return weights_ref[shard % 2, shard // 2, :, down_cols:]

    z = jnp.zeros((tokens, RANK), F32)
    p_ext = jnp.zeros((tokens, RANK + TAIL), F32)
    gram = jnp.zeros((RANK + TAIL, RANK + TAIL), F32)
    for f in range(shards):
        z += nt(x_ref[:, f * down_cols : (f + 1) * down_cols], down(f))
        cols = slice(f * up_cols, (f + 1) * up_cols)
        b_ext = jnp.concatenate([up(f), rows_ref[:, cols]], axis=0)
        p_ext += nt(r_ref[:, cols], b_ext)
        gram += nt(b_ext, b_ext)
    squares = squares_ref[:, :1]

    z16 = z.astype(BF16)
    zf = z16.astype(F32)
    p = p_ext[:, :RANK]
    m_high, m_middle, m_low = split_three(gram[:RANK, :RANK])
    v = p + (nn(z16, m_high) + (nn(z16, m_middle) + nn(z16, m_low)))
    bw = jnp.sum(gram[RANK : RANK + 3, :RANK], axis=0, keepdims=True)
    rw = jnp.sum(p_ext[:, RANK : RANK + 3], axis=1, keepdims=True)
    total = squares + jnp.sum(zf * (p + v), axis=1, keepdims=True)
    along = rw + jnp.sum(zf * bw, axis=1, keepdims=True)
    scale = lax.rsqrt(total * (1.0 / width) + 1e-05)

    length = length_ref[0]
    token = lax.broadcasted_iota(jnp.int32, (tokens, 1), 0)
    over = jnp.where(token < length, 1.0 / jnp.full((tokens, 1), length, jnp.int32).astype(F32), 0.0)
    score = jnp.sum(over * scale * along, axis=0, keepdims=True)
    alpha = over * scale
    beta = over * scale * scale * scale * along * (1.0 / width)

    dz = jnp.concatenate(split_two(alpha * bw - beta * v), axis=1)
    bz = jnp.concatenate(split_two(beta * zf), axis=1)
    az = jnp.concatenate(split_two(alpha * zf), axis=1)
    az_sum = fold_rows(tn(az, jnp.ones((tokens, LANES), BF16)))
    inner = jnp.concatenate(split_two(fold_rows(tn(bz, z16))), axis=0)
    s_high, s_middle, s_low = split_three(jnp.broadcast_to(score, (TAIL, LANES)))
    tail_row = lax.broadcasted_iota(jnp.int32, (TAIL, LANES), 0)
    tail = jnp.where(
        tail_row == 0,
        s_high.astype(F32),
        jnp.where(tail_row == 1, s_middle.astype(F32), s_low.astype(F32)),
    ).astype(BF16)
    for f in range(shards):
        term_a = fold_rows(tn(dz, x_ref[:, f * down_cols : (f + 1) * down_cols])).astype(BF16)
        at = 0
        for c in range(down_cols // LANES):
            out_ref[f, at : at + RANK, :] = term_a[:, c * LANES : (c + 1) * LANES]
            at += RANK
        term_b = fold_rows(
            tn(bz, r_ref[:, f * up_cols : (f + 1) * up_cols]) + nn(inner, up(f))
        )
        for c in range(up_cols // LANES):
            panel = f * up_cols // LANES + c
            out_ref[f, at : at + RANK, :] = (
                az_sum * w_ref[panel : panel + 1] - term_b[:, c * LANES : (c + 1) * LANES]
            ).astype(BF16)
            at += RANK
        out_ref[f, at : at + TAIL, :] = tail


def power_gap(base, count):
    factor = float(np.float32(base))
    gap = jnp.float32(0.0)
    for bit in range(COUNT_BITS):
        part = jnp.float32(1.0 - factor ** (2**bit))
        gap = jnp.where((count >> bit) & 1 == 1, gap + part - gap * part, gap)
    return gap


def pull_scores(ranks_ref, terms_ref, loss_ref):
    shards = terms_ref.shape[0]
    base = terms_ref.shape[1] - TAIL
    square = (shards, LANES)
    sublane = lax.broadcasted_iota(jnp.int32, square, 0)
    lane = lax.broadcasted_iota(jnp.int32, square, 1)
    score_col = jnp.zeros(square, F32)
    score_row = jnp.zeros(square, F32)
    place_col = jnp.zeros(square, jnp.int32)
    place_row = jnp.zeros(square, jnp.int32)
    for d in range(shards):
        parts = terms_ref[d, base : base + TAIL, :].astype(F32)
        one = jnp.broadcast_to(parts[0:1] + (parts[1:2] + parts[2:3]), square)
        score_col = jnp.where(sublane == d, one, score_col)
        score_row = jnp.where(lane == d, one, score_row)
        place_col = jnp.where(sublane == ranks_ref[0, d], d, place_col)
        place_row = jnp.where(lane == ranks_ref[0, d], d, place_row)
    live = lane < shards
    after = jnp.where(live & (place_col >= place_row), 1.0, 0.0)
    weight = jnp.exp(score_col)
    tails = jnp.where(live[:1], jnp.sum(after * weight, axis=0, keepdims=True), 1.0)
    losses = jnp.where(live[:1], jnp.log(tails) - score_row[:1], 0.0)
    loss_ref[0] = jnp.sum(losses)
    return jnp.sum(after * (weight / tails), axis=1, keepdims=True) - 1.0


def weighed(pull, terms_ref, rows):
    grad = pull[:1] * terms_ref[0, rows, :].astype(F32)
    for d in range(1, terms_ref.shape[0]):
        grad += pull[d : d + 1] * terms_ref[d, rows, :].astype(F32)
    return grad


def adamw(count, grad, param, moment, second):
    one_fix = 1.0 / jnp.full(grad.shape, power_gap(0.9, count), F32)
    two_fix = 1.0 / jnp.full(grad.shape, power_gap(0.999, count), F32)
    moment = 0.9 * moment + 0.1 * grad
    second = 0.999 * second + 0.001 * grad * grad
    change = moment * one_fix / (jnp.sqrt(second * two_fix) + 1e-08) + 0.01 * param
    return param - 0.001 * change, moment, second


def panels_of(refs):
    at = 0
    for first in (0, 3):
        for c in range(refs[first].shape[2] // LANES):
            yield slice(at, at + RANK), first, slice(c * LANES, (c + 1) * LANES)
            at += RANK


def pack_weights(a_ref, b_ref, out_ref):
    cols = a_ref.shape[2]
    for copy in range(out_ref.shape[0]):
        out_ref[copy, :, :cols] = a_ref[0].astype(BF16)
        out_ref[copy, :, cols:] = b_ref[0].astype(BF16)


def pack_state(*refs):
    out_ref = refs[-1]
    for rows, first, cols in panels_of(refs[:6]):
        for i in range(3):
            out_ref[i, rows, :] = refs[first + i][0, :, cols].astype(BF16)


def update(ranks_ref, step_ref, terms_ref, *refs):
    state, out, packed_ref, loss_ref = refs[:6], refs[6:12], refs[12], refs[13]
    pull = pull_scores(ranks_ref, terms_ref, loss_ref)
    for rows, first, cols in panels_of(state):
        grad = weighed(pull, terms_ref, rows)
        old = [state[first + i][0, :, cols] for i in range(3)]
        for i, value in enumerate(adamw(step_ref[0] + 1, grad, *old)):
            out[first + i][0, :, cols] = value
            packed_ref[i, rows, :] = value.astype(BF16)


def average(theirs_ref, *refs):
    mine, out = refs[:6], refs[6:]
    for rows, first, cols in panels_of(mine):
        for i in range(3):
            out[first + i][0, :, cols] = 0.5 * (
                mine[first + i][0, :, cols] + theirs_ref[i, rows, :].astype(F32)
            )


def gradient(ranks_ref, terms_ref, grad_ref, packed_ref, loss_ref):
    pull = pull_scores(ranks_ref, terms_ref, loss_ref)
    for first in range(0, grad_ref.shape[0], RANK):
        rows = slice(first, first + RANK)
        grad = weighed(pull, terms_ref, rows)
        grad_ref[rows, :] = grad
        packed_ref[rows, :] = grad.astype(BF16)


def own_update(step_ref, grad_ref, *refs):
    state, out = refs[:6], refs[6:]
    for rows, first, cols in panels_of(state):
        old = [state[first + i][0, :, cols] for i in range(3)]
        for i, value in enumerate(adamw(step_ref[0] + 1, grad_ref[rows, :], *old)):
            out[first + i][0, :, cols] = value


def their_update(step_ref, grad_ref, state_ref, *refs):
    mine, out = refs[:6], refs[6:]
    for rows, first, cols in panels_of(mine):
        old = [state_ref[i, rows, :].astype(F32) for i in range(3)]
        grad = grad_ref[rows, :].astype(F32)
        for i, value in enumerate(adamw(step_ref[0] + 1, grad, *old)):
            out[first + i][0, :, cols] = 0.5 * (mine[first + i][0, :, cols] + value)


def call(kernel, out_shape, smem, operands, out_specs=None, cost=(0, 0)):
    many = isinstance(out_shape, (list, tuple))
    if out_specs is None:
        out_specs = [VMEM] * len(out_shape) if many else VMEM
    return pl.pallas_call(
        kernel,
        out_shape=out_shape,
        in_specs=[SMEM] * smem + [VMEM] * (len(operands) - smem),
        out_specs=out_specs,
        compiler_params=pltpu.CompilerParams(vmem_limit_bytes=16 * 2**20),
        cost_estimate=pl.CostEstimate(flops=cost[0], bytes_accessed=cost[1], transcendentals=0),
        name=kernel.__name__,
    )(*operands)


def shape(dims, dtype):
    return jax.ShapeDtypeStruct(dims, dtype)


def finish(bit, operands):
    terms, state, ranks, step = operands
    replicas = lax.axis_size("rep")
    swap = [(i, i ^ 1 << bit) for i in range(replicas)]
    rows = terms.shape[1] - TAIL
    kept = [shape(s.shape, F32) for s in state]
    loss_shape = shape((1,), F32)
    terms = lax.all_to_all(terms, "fsdp", 0, 0)
    if replicas >> bit <= FAR:
        *mine, packed, loss = call(
            update,
            kept + [shape((3, rows, LANES), BF16), loss_shape],
            2,
            (ranks, step, terms) + state,
            [VMEM] * 7 + [SMEM],
        )
        theirs = lax.ppermute(packed, "rep", swap)
        mixed = call(average, kept, 0, (theirs,) + tuple(mine))
    else:
        old = call(pack_state, shape((3, rows, LANES), BF16), 0, state)
        their_state = lax.ppermute(old, "rep", swap)
        grad, grad16, loss = call(
            gradient,
            [shape((rows, LANES), F32), shape((rows, LANES), BF16), loss_shape],
            1,
            (ranks, terms),
            [VMEM, VMEM, SMEM],
        )
        their_grad = lax.ppermute(grad16, "rep", swap)
        mine = call(
            own_update, kept, 1, (step, grad) + state, cost=(rows * LANES * 40, rows * LANES * 24)
        )
        mixed = call(their_update, kept, 1, (step, their_grad, their_state) + tuple(mine))
    new_a, new_ma, new_va, new_b, new_mb, new_vb = mixed
    return new_a, new_b, new_ma, new_va, new_mb, new_vb, loss


def with_bit(bit):

    def step(operands):
        return finish(bit, operands)

    return step


def per_device(
    features, resid, down_weight, up_weight, down_moment, down_variance, up_moment, up_variance,
    lengths, ranks, gain, head, step,
):
    shards = lax.axis_size("fsdp")
    levels = lax.axis_size("rep").bit_length() - 1
    cols = down_weight.shape[2] + up_weight.shape[2]
    rows = cols // LANES * RANK
    panels = resid.shape[1] // LANES
    state = (down_weight, down_moment, down_variance, up_weight, up_moment, up_variance)
    same_core = [list(range(core, shards, 2)) for core in range(2)]
    same_chip = [[first, first + 1] for first in range(0, shards, 2)]
    packed = call(
        pack_weights, shape((shards // 2, RANK, cols), BF16), 0, (down_weight, up_weight)
    )
    across = lax.all_to_all(packed, "fsdp", 0, 0, axis_index_groups=same_core)
    tokens, width = resid.shape
    squares, w, w_rows = call(
        prepare,
        [shape((tokens, LANES), F32), shape((panels, LANES), F32), shape((TAIL, width), BF16)],
        0,
        (resid, gain.reshape(panels, LANES), head.reshape(panels, LANES)),
        cost=(tokens * width * 4, tokens * width * 6),
    )
    weights = lax.all_gather(across, "fsdp", axis_index_groups=same_chip)
    terms = call(
        gradient_terms,
        shape((shards, rows + TAIL, LANES), BF16),
        1,
        (lengths, features, resid, weights, squares, w, w_rows),
    )
    return lax.switch(
        step[0] % levels, [with_bit(bit) for bit in range(levels)], (terms, state, ranks, step)
    )


def solution(mesh):
    rows = P(("rep", "fsdp"), None)
    cols = P("rep", None, "fsdp")
    in_specs = (rows, rows) + (cols,) * 6 + (P(("rep", "fsdp")), P("rep", None), P(), P(), P())
    out_specs = (cols,) * 6 + (P("rep"),)
    return jax.shard_map(
        per_device, mesh=mesh, in_specs=in_specs, out_specs=out_specs, check_vma=False
    )
```

```python
import jax
import jax.numpy as jnp
import numpy as np
from jax import lax
from jax.experimental import pallas as pl
from jax.experimental.pallas import tpu as pltpu
from jax.sharding import PartitionSpec as P

F32 = jnp.float32
BF16 = jnp.bfloat16
RANK = 64
LANES = 128
TAIL = 16
COUNT_BITS = 10
FAR = 2
VMEM = pl.BlockSpec(memory_space=pltpu.VMEM)
SMEM = pl.BlockSpec(memory_space=pltpu.SMEM)


def nt(left, right):
    return lax.dot_general(left, right, (((1,), (1,)), ((), ())), preferred_element_type=F32)


def tn(left, right):
    return lax.dot_general(left, right, (((0,), (0,)), ((), ())), preferred_element_type=F32)


def nn(left, right):
    return lax.dot_general(left, right, (((1,), (0,)), ((), ())), preferred_element_type=F32)


def split_two(value):
    high = value.astype(BF16)
    return high, (value - high.astype(F32)).astype(BF16)


def split_three(value):
    high = value.astype(BF16)
    rest = value - high.astype(F32)
    middle = rest.astype(BF16)
    return high, middle, (rest - middle.astype(F32)).astype(BF16)


def fold_rows(stacked):
    half = stacked.shape[0] // 2
    return stacked[:half] + stacked[half:]


def prepare(r_ref, gain_ref, head_ref, squares_ref, w_ref, rows_ref):
    tokens, width = r_ref.shape
    w = gain_ref[...].astype(F32) * head_ref[...]
    w_ref[...] = w
    parts = [part.astype(F32) for part in split_three(w)]
    row = lax.broadcasted_iota(jnp.int32, (TAIL, LANES), 0)
    squares = jnp.zeros((tokens, LANES), F32)
    for c in range(width // LANES):
        cols = slice(c * LANES, (c + 1) * LANES)
        high, middle, low = [part[c : c + 1] for part in parts]
        rows = jnp.where(row == 0, high, jnp.where(row == 1, middle, low))
        rows_ref[:, cols] = jnp.where(row < 3, rows, 0.0).astype(BF16)
        piece = r_ref[:, cols].astype(F32)
        squares += piece * piece
    squares_ref[...] = jnp.broadcast_to(jnp.sum(squares, axis=1, keepdims=True), (tokens, LANES))


def gradient_terms(length_ref, x_ref, r_ref, weights_ref, squares_ref, w_ref, rows_ref, out_ref):
    shards = out_ref.shape[0]
    tokens, width = r_ref.shape
    down_cols = x_ref.shape[1] // shards
    up_cols = width // shards

    def down(shard):
        return weights_ref[shard % 2, shard // 2, :, :down_cols]

    def up(shard):
        return weights_ref[shard % 2, shard // 2, :, down_cols:]

    z = jnp.zeros((tokens, RANK), F32)
    p_ext = jnp.zeros((tokens, RANK + TAIL), F32)
    gram = jnp.zeros((RANK + TAIL, RANK + TAIL), F32)
    for f in range(shards):
        z += nt(x_ref[:, f * down_cols : (f + 1) * down_cols], down(f))
        cols = slice(f * up_cols, (f + 1) * up_cols)
        b_ext = jnp.concatenate([up(f), rows_ref[:, cols]], axis=0)
        p_ext += nt(r_ref[:, cols], b_ext)
        gram += nt(b_ext, b_ext)
    squares = squares_ref[:, :1]

    z16 = z.astype(BF16)
    zf = z16.astype(F32)
    p = p_ext[:, :RANK]
    m_high, m_middle, m_low = split_three(gram[:RANK, :RANK])
    v = p + (nn(z16, m_high) + (nn(z16, m_middle) + nn(z16, m_low)))
    bw = jnp.sum(gram[RANK : RANK + 3, :RANK], axis=0, keepdims=True)
    rw = jnp.sum(p_ext[:, RANK : RANK + 3], axis=1, keepdims=True)
    total = jnp.maximum(squares + jnp.sum(zf * (p + v), axis=1, keepdims=True), 0.0)
    along = rw + jnp.sum(zf * bw, axis=1, keepdims=True)
    scale = lax.rsqrt(total * (1.0 / width) + 1e-05)

    length = length_ref[0]
    token = lax.broadcasted_iota(jnp.int32, (tokens, 1), 0)
    over = jnp.where(token < length, 1.0 / jnp.full((tokens, 1), length, jnp.int32).astype(F32), 0.0)
    score = jnp.sum(over * scale * along, axis=0, keepdims=True)
    alpha = over * scale
    beta = over * scale * scale * scale * along * (1.0 / width)

    dz = jnp.concatenate(split_two(alpha * bw - beta * v), axis=1)
    bz = jnp.concatenate(split_two(beta * zf), axis=1)
    az = jnp.concatenate(split_two(alpha * zf), axis=1)
    az_sum = fold_rows(tn(az, jnp.ones((tokens, LANES), BF16)))
    inner = jnp.concatenate(split_two(fold_rows(tn(bz, z16))), axis=0)
    s_high, s_middle, s_low = split_three(jnp.broadcast_to(score, (TAIL, LANES)))
    tail_row = lax.broadcasted_iota(jnp.int32, (TAIL, LANES), 0)
    tail = jnp.where(
        tail_row == 0,
        s_high.astype(F32),
        jnp.where(tail_row == 1, s_middle.astype(F32), s_low.astype(F32)),
    ).astype(BF16)
    for f in range(shards):
        term_a = fold_rows(tn(dz, x_ref[:, f * down_cols : (f + 1) * down_cols])).astype(BF16)
        at = 0
        for c in range(down_cols // LANES):
            out_ref[f, at : at + RANK, :] = term_a[:, c * LANES : (c + 1) * LANES]
            at += RANK
        term_b = fold_rows(
            tn(bz, r_ref[:, f * up_cols : (f + 1) * up_cols]) + nn(inner, up(f))
        )
        for c in range(up_cols // LANES):
            panel = f * up_cols // LANES + c
            out_ref[f, at : at + RANK, :] = (
                az_sum * w_ref[panel : panel + 1] - term_b[:, c * LANES : (c + 1) * LANES]
            ).astype(BF16)
            at += RANK
        out_ref[f, at : at + TAIL, :] = tail


def power_gap(base, count):
    factor = float(np.float32(base))
    gap = jnp.float32(0.0)
    for bit in range(COUNT_BITS):
        part = jnp.float32(1.0 - factor ** (2**bit))
        gap = jnp.where((count >> bit) & 1 == 1, gap + part - gap * part, gap)
    return gap


def pull_scores(ranks_ref, terms_ref, loss_ref):
    shards = terms_ref.shape[0]
    base = terms_ref.shape[1] - TAIL
    square = (shards, LANES)
    sublane = lax.broadcasted_iota(jnp.int32, square, 0)
    lane = lax.broadcasted_iota(jnp.int32, square, 1)
    score_col = jnp.zeros(square, F32)
    score_row = jnp.zeros(square, F32)
    place_col = jnp.zeros(square, jnp.int32)
    place_row = jnp.zeros(square, jnp.int32)
    for d in range(shards):
        parts = terms_ref[d, base : base + TAIL, :].astype(F32)
        one = jnp.broadcast_to(parts[0:1] + (parts[1:2] + parts[2:3]), square)
        score_col = jnp.where(sublane == d, one, score_col)
        score_row = jnp.where(lane == d, one, score_row)
        place_col = jnp.where(sublane == ranks_ref[0, d], d, place_col)
        place_row = jnp.where(lane == ranks_ref[0, d], d, place_row)
    live = lane < shards
    after = jnp.where(live & (place_col >= place_row), 1.0, 0.0)
    weight = jnp.exp(score_col)
    tails = jnp.where(live[:1], jnp.sum(after * weight, axis=0, keepdims=True), 1.0)
    losses = jnp.where(live[:1], jnp.log(tails) - score_row[:1], 0.0)
    loss_ref[...] = jnp.broadcast_to(jnp.sum(losses, axis=1, keepdims=True), loss_ref.shape)
    return jnp.sum(after * (weight / tails), axis=1, keepdims=True) - 1.0


def weighed(pull, terms_ref, rows):
    grad = pull[:1] * terms_ref[0, rows, :].astype(F32)
    for d in range(1, terms_ref.shape[0]):
        grad += pull[d : d + 1] * terms_ref[d, rows, :].astype(F32)
    return grad


def adamw(count, grad, param, moment, second):
    one_fix = 1.0 / jnp.full(grad.shape, power_gap(0.9, count), F32)
    two_fix = 1.0 / jnp.full(grad.shape, power_gap(0.999, count), F32)
    moment = 0.9 * moment + 0.1 * grad
    second = 0.999 * second + 0.001 * grad * grad
    change = moment * one_fix / (jnp.sqrt(second * two_fix) + 1e-08) + 0.01 * param
    return param - 0.001 * change, moment, second


def panels_of(refs):
    at = 0
    for first in (0, 3):
        for c in range(refs[first].shape[2] // LANES):
            yield slice(at, at + RANK), first, slice(c * LANES, (c + 1) * LANES)
            at += RANK


def pack_weights(a_ref, b_ref, out_ref):
    cols = a_ref.shape[2]
    for copy in range(out_ref.shape[0]):
        out_ref[copy, :, :cols] = a_ref[0].astype(BF16)
        out_ref[copy, :, cols:] = b_ref[0].astype(BF16)


def pack_state(*refs):
    out_ref = refs[-1]
    for rows, first, cols in panels_of(refs[:6]):
        for i in range(3):
            out_ref[i, rows, :] = refs[first + i][0, :, cols].astype(out_ref.dtype)


def update(ranks_ref, step_ref, terms_ref, *refs):
    state, out, packed_ref, loss_ref = refs[:6], refs[6:12], refs[12], refs[13]
    pull = pull_scores(ranks_ref, terms_ref, loss_ref)
    for rows, first, cols in panels_of(state):
        grad = weighed(pull, terms_ref, rows)
        old = [state[first + i][0, :, cols] for i in range(3)]
        for i, value in enumerate(adamw(step_ref[0] + 1, grad, *old)):
            out[first + i][0, :, cols] = value
            packed_ref[i, rows, :] = value.astype(BF16)


def average(theirs_ref, loss_tile_ref, *refs):
    mine, out, loss_ref = refs[:6], refs[6:12], refs[12]
    loss_ref[0] = loss_tile_ref[0, 0]
    for rows, first, cols in panels_of(mine):
        for i in range(3):
            out[first + i][0, :, cols] = 0.5 * (
                mine[first + i][0, :, cols] + theirs_ref[i, rows, :].astype(F32)
            )


def gradient(ranks_ref, terms_ref, grad_ref, packed_ref, loss_ref):
    pull = pull_scores(ranks_ref, terms_ref, loss_ref)
    for first in range(0, grad_ref.shape[0], RANK):
        rows = slice(first, first + RANK)
        grad = weighed(pull, terms_ref, rows)
        grad_ref[rows, :] = grad
        packed_ref[rows, :] = grad.astype(BF16)


def own_update(step_ref, grad_ref, loss_tile_ref, *refs):
    state, out, loss_ref = refs[:6], refs[6:12], refs[12]
    loss_ref[0] = loss_tile_ref[0, 0]
    for rows, first, cols in panels_of(state):
        old = [state[first + i][0, :, cols] for i in range(3)]
        for i, value in enumerate(adamw(step_ref[0] + 1, grad_ref[rows, :], *old)):
            out[first + i][0, :, cols] = value


def their_update(step_ref, grad_ref, state_ref, *refs):
    mine, out = refs[:6], refs[6:]
    for rows, first, cols in panels_of(mine):
        old = [state_ref[i, rows, :].astype(F32) for i in range(3)]
        grad = grad_ref[rows, :].astype(F32)
        for i, value in enumerate(adamw(step_ref[0] + 1, grad, *old)):
            out[first + i][0, :, cols] = 0.5 * (mine[first + i][0, :, cols] + value)


def call(kernel, out_shape, smem, operands, out_specs=None, cost=(0, 0)):
    many = isinstance(out_shape, (list, tuple))
    if out_specs is None:
        out_specs = [VMEM] * len(out_shape) if many else VMEM
    return pl.pallas_call(
        kernel,
        out_shape=out_shape,
        in_specs=[SMEM] * smem + [VMEM] * (len(operands) - smem),
        out_specs=out_specs,
        compiler_params=pltpu.CompilerParams(vmem_limit_bytes=16 * 2**20),
        cost_estimate=pl.CostEstimate(flops=cost[0], bytes_accessed=cost[1], transcendentals=0),
        name=kernel.__name__,
    )(*operands)


def shape(dims, dtype):
    return jax.ShapeDtypeStruct(dims, dtype)


def finish(bit, operands):
    terms, state, ranks, step = operands
    replicas = lax.axis_size("rep")
    swap = [(i, i ^ 1 << bit) for i in range(replicas)]
    rows = terms.shape[1] - TAIL
    kept = [shape(s.shape, F32) for s in state]
    loss_shape = shape((1,), F32)
    loss_tile = shape((8, LANES), F32)
    terms = lax.all_to_all(terms, "fsdp", 0, 0)
    if replicas >> bit <= FAR:
        *mine, packed, loss = call(
            update,
            kept + [shape((3, rows, LANES), BF16), loss_tile],
            2,
            (ranks, step, terms) + state,
        )
        theirs = lax.ppermute(packed, "rep", swap)
        *mixed, loss = call(
            average, kept + [loss_shape], 0, (theirs, loss) + tuple(mine), [VMEM] * 6 + [SMEM]
        )
    else:
        kind = BF16 if replicas >> bit <= 2 * FAR else F32
        old = call(pack_state, shape((3, rows, LANES), kind), 0, state)
        their_state = lax.ppermute(old, "rep", swap)
        grad, grad16, loss = call(
            gradient,
            [shape((rows, LANES), F32), shape((rows, LANES), BF16), loss_tile],
            1,
            (ranks, terms),
        )
        their_grad = lax.ppermute(grad16, "rep", swap)
        *mine, loss = call(
            own_update,
            kept + [loss_shape],
            1,
            (step, grad, loss) + state,
            [VMEM] * 6 + [SMEM],
            cost=(rows * LANES * 40, rows * LANES * 24),
        )
        mixed = call(their_update, kept, 1, (step, their_grad, their_state) + tuple(mine))
    new_a, new_ma, new_va, new_b, new_mb, new_vb = mixed
    return new_a, new_b, new_ma, new_va, new_mb, new_vb, loss


def with_bit(bit):

    def step(operands):
        return finish(bit, operands)

    return step


def per_device(
    features, resid, down_weight, up_weight, down_moment, down_variance, up_moment, up_variance,
    lengths, ranks, gain, head, step,
):
    shards = lax.axis_size("fsdp")
    levels = lax.axis_size("rep").bit_length() - 1
    cols = down_weight.shape[2] + up_weight.shape[2]
    rows = cols // LANES * RANK
    panels = resid.shape[1] // LANES
    state = (down_weight, down_moment, down_variance, up_weight, up_moment, up_variance)
    same_core = [list(range(core, shards, 2)) for core in range(2)]
    same_chip = [[first, first + 1] for first in range(0, shards, 2)]
    packed = call(
        pack_weights, shape((shards // 2, RANK, cols), BF16), 0, (down_weight, up_weight)
    )
    across = lax.all_to_all(packed, "fsdp", 0, 0, axis_index_groups=same_core)
    tokens, width = resid.shape
    squares, w, w_rows = call(
        prepare,
        [shape((tokens, LANES), F32), shape((panels, LANES), F32), shape((TAIL, width), BF16)],
        0,
        (resid, gain.reshape(panels, LANES), head.reshape(panels, LANES)),
        cost=(tokens * width * 4, tokens * width * 6),
    )
    weights = lax.all_gather(across, "fsdp", axis_index_groups=same_chip)
    terms = call(
        gradient_terms,
        shape((shards, rows + TAIL, LANES), BF16),
        1,
        (lengths, features, resid, weights, squares, w, w_rows),
    )
    return lax.switch(
        step[0] % levels, [with_bit(bit) for bit in range(levels)], (terms, state, ranks, step)
    )


def solution(mesh):
    rows = P(("rep", "fsdp"), None)
    cols = P("rep", None, "fsdp")
    in_specs = (rows, rows) + (cols,) * 6 + (P(("rep", "fsdp")), P("rep", None), P(), P(), P())
    out_specs = (cols,) * 6 + (P("rep"),)
    return jax.shard_map(
        per_device, mesh=mesh, in_specs=in_specs, out_specs=out_specs, check_vma=False
    )
```

```python
import jax
import jax.numpy as jnp
import numpy as np
from jax import lax
from jax.experimental import pallas as pl
from jax.experimental.pallas import tpu as pltpu
from jax.sharding import PartitionSpec as P

F32 = jnp.float32
BF16 = jnp.bfloat16
RANK = 64
LANES = 128
TAIL = 16
COUNT_BITS = 10
FAR = 2
VMEM = pl.BlockSpec(memory_space=pltpu.VMEM)
SMEM = pl.BlockSpec(memory_space=pltpu.SMEM)


def nt(left, right):
    return lax.dot_general(left, right, (((1,), (1,)), ((), ())), preferred_element_type=F32)


def tn(left, right):
    return lax.dot_general(left, right, (((0,), (0,)), ((), ())), preferred_element_type=F32)


def nn(left, right):
    return lax.dot_general(left, right, (((1,), (0,)), ((), ())), preferred_element_type=F32)


def split_two(value):
    high = value.astype(BF16)
    return high, (value - high.astype(F32)).astype(BF16)


def split_three(value):
    high = value.astype(BF16)
    rest = value - high.astype(F32)
    middle = rest.astype(BF16)
    return high, middle, (rest - middle.astype(F32)).astype(BF16)


def fold_rows(stacked):
    half = stacked.shape[0] // 2
    return stacked[:half] + stacked[half:]


def prepare(r_ref, gain_ref, head_ref, squares_ref, w_ref, rows_ref):
    tokens, width = r_ref.shape
    w = gain_ref[...].astype(F32) * head_ref[...]
    w_ref[...] = w
    parts = [part.astype(F32) for part in split_three(w)]
    row = lax.broadcasted_iota(jnp.int32, (TAIL, LANES), 0)
    squares = jnp.zeros((tokens, LANES), F32)
    for c in range(width // LANES):
        cols = slice(c * LANES, (c + 1) * LANES)
        high, middle, low = [part[c : c + 1] for part in parts]
        rows = jnp.where(row == 0, high, jnp.where(row == 1, middle, low))
        rows_ref[:, cols] = jnp.where(row < 3, rows, 0.0).astype(BF16)
        piece = r_ref[:, cols].astype(F32)
        squares += piece * piece
    squares_ref[...] = jnp.broadcast_to(jnp.sum(squares, axis=1, keepdims=True), (tokens, LANES))


def gradient_terms(length_ref, x_ref, r_ref, weights_ref, squares_ref, w_ref, rows_ref, out_hbm, out_ref, sems):
    shards = out_ref.shape[0]
    tokens, width = r_ref.shape
    down_cols = x_ref.shape[1] // shards
    up_cols = width // shards

    def down(shard):
        return weights_ref[shard % 2, shard // 2, :, :down_cols]

    def up(shard):
        return weights_ref[shard % 2, shard // 2, :, down_cols:]

    z = jnp.zeros((tokens, RANK), F32)
    p_ext = jnp.zeros((tokens, RANK + TAIL), F32)
    gram = jnp.zeros((RANK + TAIL, RANK + TAIL), F32)
    for f in range(shards):
        z += nt(x_ref[:, f * down_cols : (f + 1) * down_cols], down(f))
        cols = slice(f * up_cols, (f + 1) * up_cols)
        b_ext = jnp.concatenate([up(f), rows_ref[:, cols]], axis=0)
        p_ext += nt(r_ref[:, cols], b_ext)
        gram += nt(b_ext, b_ext)
    squares = squares_ref[:, :1]

    z16 = z.astype(BF16)
    zf = z16.astype(F32)
    p = p_ext[:, :RANK]
    m_high, m_low = split_two(gram[:RANK, :RANK])
    v = p + (nn(z16, m_high) + nn(z16, m_low))
    bw = jnp.sum(gram[RANK : RANK + 3, :RANK], axis=0, keepdims=True)
    rw = jnp.sum(p_ext[:, RANK : RANK + 3], axis=1, keepdims=True)
    total = jnp.maximum(squares + jnp.sum(zf * (p + v), axis=1, keepdims=True), 0.0)
    along = rw + jnp.sum(zf * bw, axis=1, keepdims=True)
    scale = lax.rsqrt(total * (1.0 / width) + 1e-05)

    length = length_ref[0]
    token = lax.broadcasted_iota(jnp.int32, (tokens, 1), 0)
    over = jnp.where(token < length, 1.0 / jnp.full((tokens, 1), length, jnp.int32).astype(F32), 0.0)
    score = jnp.sum(over * scale * along, axis=0, keepdims=True)
    alpha = over * scale
    beta = over * scale * scale * scale * along * (1.0 / width)

    dz = jnp.concatenate(split_two(alpha * bw - beta * v), axis=1)
    bz = jnp.concatenate(split_two(beta * zf), axis=1)
    az = jnp.concatenate(split_two(alpha * zf), axis=1)
    az_sum = fold_rows(tn(az, jnp.ones((tokens, LANES), BF16)))
    inner = jnp.concatenate(split_two(fold_rows(tn(bz, z16))), axis=0)
    s_high, s_middle, s_low = split_three(jnp.broadcast_to(score, (TAIL, LANES)))
    tail_row = lax.broadcasted_iota(jnp.int32, (TAIL, LANES), 0)
    tail = jnp.where(
        tail_row == 0,
        s_high.astype(F32),
        jnp.where(tail_row == 1, s_middle.astype(F32), s_low.astype(F32)),
    ).astype(BF16)
    for f in range(shards):
        term_a = fold_rows(tn(dz, x_ref[:, f * down_cols : (f + 1) * down_cols])).astype(BF16)
        at = 0
        for c in range(down_cols // LANES):
            out_ref[f, at : at + RANK, :] = term_a[:, c * LANES : (c + 1) * LANES]
            at += RANK
        term_b = fold_rows(
            tn(bz, r_ref[:, f * up_cols : (f + 1) * up_cols]) + nn(inner, up(f))
        )
        for c in range(up_cols // LANES):
            panel = f * up_cols // LANES + c
            out_ref[f, at : at + RANK, :] = (
                az_sum * w_ref[panel : panel + 1] - term_b[:, c * LANES : (c + 1) * LANES]
            ).astype(BF16)
            at += RANK
        out_ref[f, at : at + TAIL, :] = tail
        if f == shards - 3:
            early = pltpu.make_async_copy(
                out_ref.at[: shards - 2], out_hbm.at[: shards - 2], sems.at[0]
            )
            early.start()
    late = pltpu.make_async_copy(out_ref.at[shards - 2 :], out_hbm.at[shards - 2 :], sems.at[1])
    late.start()
    early.wait()
    late.wait()


def power_gap(base, count):
    factor = float(np.float32(base))
    gap = jnp.float32(0.0)
    for bit in range(COUNT_BITS):
        part = jnp.float32(1.0 - factor ** (2**bit))
        gap = jnp.where((count >> bit) & 1 == 1, gap + part - gap * part, gap)
    return gap


def pull_scores(ranks_ref, terms_ref, loss_ref):
    shards = terms_ref.shape[0]
    base = terms_ref.shape[1] - TAIL
    square = (shards, LANES)
    sublane = lax.broadcasted_iota(jnp.int32, square, 0)
    lane = lax.broadcasted_iota(jnp.int32, square, 1)
    score_col = jnp.zeros(square, F32)
    score_row = jnp.zeros(square, F32)
    place_col = jnp.zeros(square, jnp.int32)
    place_row = jnp.zeros(square, jnp.int32)
    for d in range(shards):
        parts = terms_ref[d, base : base + TAIL, :].astype(F32)
        one = jnp.broadcast_to(parts[0:1] + (parts[1:2] + parts[2:3]), square)
        score_col = jnp.where(sublane == d, one, score_col)
        score_row = jnp.where(lane == d, one, score_row)
        place_col = jnp.where(sublane == ranks_ref[0, d], d, place_col)
        place_row = jnp.where(lane == ranks_ref[0, d], d, place_row)
    live = lane < shards
    after = jnp.where(live & (place_col >= place_row), 1.0, 0.0)
    weight = jnp.exp(score_col)
    tails = jnp.where(live[:1], jnp.sum(after * weight, axis=0, keepdims=True), 1.0)
    losses = jnp.where(live[:1], jnp.log(tails) - score_row[:1], 0.0)
    loss_ref[...] = jnp.broadcast_to(jnp.sum(losses, axis=1, keepdims=True), loss_ref.shape)
    return jnp.sum(after * (weight / tails), axis=1, keepdims=True) - 1.0


def weighed(pull, terms_ref, rows):
    grad = pull[:1] * terms_ref[0, rows, :].astype(F32)
    for d in range(1, terms_ref.shape[0]):
        grad += pull[d : d + 1] * terms_ref[d, rows, :].astype(F32)
    return grad


def adamw(count, grad, param, moment, second):
    one_fix = 1.0 / jnp.full(grad.shape, power_gap(0.9, count), F32)
    two_fix = 1.0 / jnp.full(grad.shape, power_gap(0.999, count), F32)
    moment = 0.9 * moment + 0.1 * grad
    second = 0.999 * second + 0.001 * grad * grad
    change = moment * one_fix / (jnp.sqrt(second * two_fix) + 1e-08) + 0.01 * param
    return param - 0.001 * change, moment, second


def panels_of(refs):
    at = 0
    for first in (0, 3):
        for c in range(refs[first].shape[2] // LANES):
            yield slice(at, at + RANK), first, slice(c * LANES, (c + 1) * LANES)
            at += RANK


def pack_weights(a_ref, b_ref, out_ref):
    cols = a_ref.shape[2]
    for copy in range(out_ref.shape[0]):
        out_ref[copy, :, :cols] = a_ref[0].astype(BF16)
        out_ref[copy, :, cols:] = b_ref[0].astype(BF16)


def pack_state(*refs):
    out_ref = refs[-1]
    for rows, first, cols in panels_of(refs[:6]):
        for i in range(3):
            out_ref[i, rows, :] = refs[first + i][0, :, cols].astype(out_ref.dtype)


def update(ranks_ref, step_ref, terms_ref, *refs):
    state, out, packed_ref, loss_ref = refs[:6], refs[6:12], refs[12], refs[13]
    pull = pull_scores(ranks_ref, terms_ref, loss_ref)
    for rows, first, cols in panels_of(state):
        grad = weighed(pull, terms_ref, rows)
        old = [state[first + i][0, :, cols] for i in range(3)]
        for i, value in enumerate(adamw(step_ref[0] + 1, grad, *old)):
            out[first + i][0, :, cols] = value
            packed_ref[i, rows, :] = value.astype(BF16)


def average(theirs_ref, loss_tile_ref, *refs):
    mine, out, loss_ref = refs[:6], refs[6:12], refs[12]
    loss_ref[0] = loss_tile_ref[0, 0]
    for rows, first, cols in panels_of(mine):
        for i in range(3):
            out[first + i][0, :, cols] = 0.5 * (
                mine[first + i][0, :, cols] + theirs_ref[i, rows, :].astype(F32)
            )


def gradient(ranks_ref, terms_ref, grad_ref, packed_ref, loss_ref):
    pull = pull_scores(ranks_ref, terms_ref, loss_ref)
    for first in range(0, grad_ref.shape[0], RANK):
        rows = slice(first, first + RANK)
        grad = weighed(pull, terms_ref, rows)
        grad_ref[rows, :] = grad
        packed_ref[rows, :] = grad.astype(BF16)


def own_update(step_ref, grad_ref, loss_tile_ref, *refs):
    state, out, loss_ref = refs[:6], refs[6:12], refs[12]
    loss_ref[0] = loss_tile_ref[0, 0]
    for rows, first, cols in panels_of(state):
        old = [state[first + i][0, :, cols] for i in range(3)]
        for i, value in enumerate(adamw(step_ref[0] + 1, grad_ref[rows, :], *old)):
            out[first + i][0, :, cols] = value


def their_update(step_ref, grad_ref, state_ref, *refs):
    mine, out = refs[:6], refs[6:]
    for rows, first, cols in panels_of(mine):
        old = [state_ref[i, rows, :].astype(F32) for i in range(3)]
        grad = grad_ref[rows, :].astype(F32)
        for i, value in enumerate(adamw(step_ref[0] + 1, grad, *old)):
            out[first + i][0, :, cols] = 0.5 * (mine[first + i][0, :, cols] + value)


def call(kernel, out_shape, smem, operands, out_specs=None, cost=(0, 0), scratch=()):
    many = isinstance(out_shape, (list, tuple))
    if out_specs is None:
        out_specs = [VMEM] * len(out_shape) if many else VMEM
    return pl.pallas_call(
        kernel,
        out_shape=out_shape,
        in_specs=[SMEM] * smem + [VMEM] * (len(operands) - smem),
        out_specs=out_specs,
        scratch_shapes=scratch,
        compiler_params=pltpu.CompilerParams(vmem_limit_bytes=16 * 2**20),
        cost_estimate=pl.CostEstimate(flops=cost[0], bytes_accessed=cost[1], transcendentals=0),
        name=kernel.__name__,
    )(*operands)


def shape(dims, dtype):
    return jax.ShapeDtypeStruct(dims, dtype)


def finish(bit, operands):
    terms, state, ranks, step = operands
    replicas = lax.axis_size("rep")
    swap = [(i, i ^ 1 << bit) for i in range(replicas)]
    rows = terms.shape[1] - TAIL
    kept = [shape(s.shape, F32) for s in state]
    loss_shape = shape((1,), F32)
    loss_tile = shape((8, LANES), F32)
    terms = lax.all_to_all(terms, "fsdp", 0, 0)
    if replicas >> bit <= FAR:
        *mine, packed, loss = call(
            update,
            kept + [shape((3, rows, LANES), BF16), loss_tile],
            2,
            (ranks, step, terms) + state,
        )
        theirs = lax.ppermute(packed, "rep", swap)
        *mixed, loss = call(
            average, kept + [loss_shape], 0, (theirs, loss) + tuple(mine), [VMEM] * 6 + [SMEM]
        )
    else:
        kind = BF16 if replicas >> bit <= 2 * FAR else F32
        old = call(pack_state, shape((3, rows, LANES), kind), 0, state)
        their_state = lax.ppermute(old, "rep", swap)
        grad, grad16, loss = call(
            gradient,
            [shape((rows, LANES), F32), shape((rows, LANES), BF16), loss_tile],
            1,
            (ranks, terms),
        )
        their_grad = lax.ppermute(grad16, "rep", swap)
        *mine, loss = call(
            own_update,
            kept + [loss_shape],
            1,
            (step, grad, loss) + state,
            [VMEM] * 6 + [SMEM],
            cost=(rows * LANES * 40, rows * LANES * 24),
        )
        mixed = call(their_update, kept, 1, (step, their_grad, their_state) + tuple(mine))
    new_a, new_ma, new_va, new_b, new_mb, new_vb = mixed
    return new_a, new_b, new_ma, new_va, new_mb, new_vb, loss


def with_bit(bit):

    def step(operands):
        return finish(bit, operands)

    return step


def per_device(
    features, resid, down_weight, up_weight, down_moment, down_variance, up_moment, up_variance,
    lengths, ranks, gain, head, step,
):
    shards = lax.axis_size("fsdp")
    levels = lax.axis_size("rep").bit_length() - 1
    cols = down_weight.shape[2] + up_weight.shape[2]
    rows = cols // LANES * RANK
    panels = resid.shape[1] // LANES
    state = (down_weight, down_moment, down_variance, up_weight, up_moment, up_variance)
    same_core = [list(range(core, shards, 2)) for core in range(2)]
    same_chip = [[first, first + 1] for first in range(0, shards, 2)]
    packed = call(
        pack_weights, shape((shards // 2, RANK, cols), BF16), 0, (down_weight, up_weight)
    )
    across = lax.all_to_all(packed, "fsdp", 0, 0, axis_index_groups=same_core)
    tokens, width = resid.shape
    squares, w, w_rows = call(
        prepare,
        [shape((tokens, LANES), F32), shape((panels, LANES), F32), shape((TAIL, width), BF16)],
        0,
        (resid, gain.reshape(panels, LANES), head.reshape(panels, LANES)),
        cost=(tokens * width * 4, tokens * width * 6),
    )
    weights = lax.all_gather(across, "fsdp", axis_index_groups=same_chip)
    terms = call(
        gradient_terms,
        shape((shards, rows + TAIL, LANES), BF16),
        1,
        (lengths, features, resid, weights, squares, w, w_rows),
        pl.BlockSpec(memory_space=pl.ANY),
        scratch=[
            pltpu.VMEM((shards, rows + TAIL, LANES), BF16), pltpu.SemaphoreType.DMA((2,)),
        ],
    )
    return lax.switch(
        step[0] % levels, [with_bit(bit) for bit in range(levels)], (terms, state, ranks, step)
    )


def solution(mesh):
    rows = P(("rep", "fsdp"), None)
    cols = P("rep", None, "fsdp")
    in_specs = (rows, rows) + (cols,) * 6 + (P(("rep", "fsdp")), P("rep", None), P(), P(), P())
    out_specs = (cols,) * 6 + (P("rep"),)
    return jax.shard_map(
        per_device, mesh=mesh, in_specs=in_specs, out_specs=out_specs, check_vma=False
    )
```
